32 devices in a mesh: groups: 2 (over y), seq: 8 (over z, x), tp: 2 (over core).
Axes of the slice: x: 2, y: 2, z: 4, core: 2. Of those that a mesh axis runs over, the one named last changes fastest.
Arguments:
- query_rows: bfloat16 [2048, 4096], P(('groups', 'seq'), 'tp'), parts along dimension 0, may hold values from -1.78125 to 1.78125
- key_rows: bfloat16 [2048, 4096], P(('groups', 'seq'), 'tp'), parts along dimension 0, may hold values from -1.78125 to 1.78125
- value_rows: bfloat16 [2048, 4096], P(('groups', 'seq'), 'tp'), parts along dimension 0, may hold values from -180 to 180
- log_decay: float32 [32, 2048], P('tp', ('groups', 'seq')), parts along dimension 1, may hold values from -2 to 0
- carried_state: bfloat16 [64, 128, 128], P(('groups', 'tp')), parts along dimension 0, may hold values from -48 to 48
- norm_gain: float32 [4096], P('tp'), may hold values from 0.1 to 1.9
Outputs:
- attention_out: bfloat16 [2048, 4096], P(('groups', 'seq'), 'tp'), parts along dimension 0
The draws below stay inside these ranges and needn't reach their ends.
There are 2 independent parts, one for each index of `groups`. The reference program is written for one: setup_inputs(seed, part) draws one part's arguments, and reference() takes and returns one part's arrays. A program takes and returns all parts, laid end to end along the dimension named above; an argument that names none is the same for every part. Nothing has to cross between parts.
All inputs are finite; a program needn't handle non-finite values.
Results may differ from the reference program's by a relative error of at most 0.007.
Values may be sent and summed in bfloat16 or wider, within the bound.
A program may use at most 256 MiB of HBM per device.

```python
import math
import jax
import jax.numpy as jnp
from jax import lax

LOCAL_HEADS = 32
DH = 128
TOK_DEV = 128
WINDOW_TOKENS = 1024
N_SEQ = 8


def draw_log_decay(key, part):
    key = jax.random.fold_in(key, 11)
    key_collection = jax.random.split(key, 7)
    fast_share = 0.5
    picker = jax.random.uniform(key_collection[0], (LOCAL_HEADS,))
    fast_rate = jax.random.uniform(key_collection[1], (LOCAL_HEADS,), minval=1.0 / 50.0, maxval=1.0 / 30.0)
    slow_rate = jnp.exp(jax.random.uniform(key_collection[2], (LOCAL_HEADS,), minval=math.log(0.1), maxval=math.log(0.5))) / WINDOW_TOKENS
    rate = jnp.where(picker < fast_share, fast_rate, slow_rate)
    jitter = jnp.exp(jax.random.uniform(key_collection[3], (WINDOW_TOKENS, LOCAL_HEADS), minval=-0.35, maxval=0.35))
    block_factor = jnp.exp(jax.random.uniform(key_collection[4], (WINDOW_TOKENS // TOK_DEV, LOCAL_HEADS), minval=-0.35, maxval=0.35))
    block_factor = jnp.repeat(block_factor, TOK_DEV, axis=0)
    value_entries = -rate[None] * jitter * block_factor
    segment_offset = jax.random.randint(key_collection[5], (3, LOCAL_HEADS), 0, WINDOW_TOKENS)
    segment_length = jax.random.uniform(key_collection[6], (3, LOCAL_HEADS), minval=math.log(0.6), maxval=math.log(0.8))
    token_places = jnp.arange(WINDOW_TOKENS)[:, None, None]
    value_entries = value_entries + jnp.sum(jnp.where(token_places == segment_offset[None], segment_length[None], 0.0), axis=1)
    return value_entries.T.astype(jnp.float32)


def draw_value_rows(key, part):
    key = jax.random.fold_in(key, 23)
    key_collection = jax.random.split(key, 2)
    head_of = jnp.arange(LOCAL_HEADS * DH) // DH
    column_scale = 10.0 ** (head_of.astype(jnp.float32) / max(LOCAL_HEADS - 1, 1))
    row_scale = jnp.exp(jax.random.uniform(key_collection[0], (WINDOW_TOKENS, 1), minval=0.0, maxval=math.log(10.0)))
    base = jnp.clip(jax.random.normal(key_collection[1], (WINDOW_TOKENS, LOCAL_HEADS * DH)), -6.0, 6.0)
    return (0.3 * base * row_scale * column_scale[None]).astype(jnp.bfloat16)


def levels(stream_key, extent, shards, least, high):
    def one(position, blocks):
        steps = jax.random.uniform(jax.random.fold_in(jax.random.fold_in(stream_key, 6), position), (blocks,), jnp.float32, least / len(shards), high / len(shards))
        return jnp.repeat(jnp.exp(steps), extent[position] // blocks).reshape((-1,) + (1,) * (len(extent) - position - 1))

    factor_of = one(*shards[0])
    for cut in shards[1:]:
        factor_of = factor_of * one(*cut)
    return factor_of


def normal_values(key, shape, deviation, bound, cuts=(), held_as=jnp.bfloat16):
    drawn = jax.random.normal(key, shape, jnp.float32) * deviation
    if len(cuts) > 0:
        drawn = levels(key, shape, cuts, -0.22, 0.18) * drawn
    return jnp.clip(drawn, min=-bound, max=bound).astype(held_as)


def setup_inputs(seed: int = 0, part: int = 0) -> dict:
    arg_keys = jax.random.split(jax.random.key(seed), 7)
    part_keys = jax.random.split(jax.random.fold_in(arg_keys[6], part), 7)
    query_rows = normal_values(part_keys[0], (WINDOW_TOKENS, LOCAL_HEADS * DH), (DH ** -0.25), 1.78125, ((0, 8), (1, 2)))
    key_rows = normal_values(part_keys[1], (WINDOW_TOKENS, LOCAL_HEADS * DH), (DH ** -0.25), 1.78125, ((0, 8), (1, 2)))
    value_rows = draw_value_rows(jax.random.fold_in(jax.random.fold_in(arg_keys[6], part), 71), part)
    log_decay = draw_log_decay(jax.random.fold_in(jax.random.fold_in(arg_keys[6], part), 71), part)
    carried_state = normal_values(part_keys[4], (LOCAL_HEADS, DH, DH), 8.0, 48.0, ((0, 2),))
    norm_gain = jnp.clip(1.0 + 0.18 * jax.random.normal(arg_keys[5], (LOCAL_HEADS * DH,), jnp.float32), 0.1, 1.9)
    return {"query_rows": query_rows, "key_rows": key_rows, "value_rows": value_rows, "log_decay": log_decay, "carried_state": carried_state, "norm_gain": norm_gain}


def block_local(query_block, key_block, value_block, decay_block):
    head_count, row_count = decay_block.shape
    head_width = query_block.shape[1] // head_count
    query_heads = query_block.reshape(row_count, head_count, head_width).astype(jnp.float32)
    key_heads = key_block.reshape(row_count, head_count, head_width).astype(jnp.float32)
    value_heads = value_block.reshape(row_count, head_count, head_width).astype(jnp.float32)
    cumulative = jnp.cumsum(decay_block, axis=1)
    scores = jnp.einsum('thd,shd->hts', query_heads, key_heads)
    causal = jnp.tril(jnp.ones((row_count, row_count), dtype=bool))[None]
    spread = cumulative[:, :, None] - cumulative[:, None, :]
    weights = jnp.where(causal, jnp.exp(jnp.minimum(spread, 0.0)), 0.0)
    mixing = (scores * weights).astype(jnp.bfloat16)
    inside = jnp.einsum('hts,shd->thd', mixing.astype(jnp.float32), value_heads)
    block_log = cumulative[:, -1]
    key_decayed = (key_heads * jnp.exp(block_log[:, None] - cumulative).T[:, :, None]).astype(jnp.bfloat16)
    block_state = jnp.einsum('thd,the->hde', key_decayed.astype(jnp.float32), value_heads).astype(jnp.bfloat16)
    query_decayed = (query_heads * jnp.exp(cumulative).T[:, :, None]).astype(jnp.bfloat16)
    return (inside, query_decayed, block_state, block_log)

def reference(query_rows, key_rows, value_rows, log_decay, carried_state, norm_gain):
    feature_count = query_rows.shape[1]
    head_total = log_decay.shape[0]
    blocks = (query_rows.reshape(N_SEQ, TOK_DEV, feature_count), key_rows.reshape(N_SEQ, TOK_DEV, feature_count), value_rows.reshape(N_SEQ, TOK_DEV, feature_count), jnp.transpose(log_decay.reshape(head_total, N_SEQ, TOK_DEV), (1, 0, 2)))

    def advance(memory, block):
        inside, query_decayed, block_state, block_log = block_local(*block)
        entering = memory.astype(jnp.bfloat16)
        outside = jnp.einsum('thd,hde->the', query_decayed.astype(jnp.float32), entering.astype(jnp.float32))
        combined = (inside + outside).reshape(TOK_DEV, feature_count)
        meansq = lax.optimization_barrier(jnp.mean(combined * combined, axis=1))
        result = (combined * lax.rsqrt(meansq + 1e-06)[:, None] * norm_gain[None]).astype(jnp.bfloat16)
        updated = jnp.exp(block_log)[:, None, None] * memory + block_state.astype(jnp.float32)
        return (updated, result)
    _, outputs = lax.scan(advance, carried_state.astype(jnp.float32), blocks)
    return outputs.reshape(WINDOW_TOKENS, feature_count)
```

```python
import functools

import jax
import jax.numpy as jnp
from jax import lax
from jax.experimental import pallas as pl
from jax.experimental.pallas import tpu as pltpu
from jax.sharding import PartitionSpec as P

MESH = pl.DeviceIdType.MESH
F32 = jnp.float32
BF16 = jnp.bfloat16
EXACT = lax.Precision.HIGHEST


def kernel(
    pairs,
    features,
    query_hbm,
    key_hbm,
    value_hbm,
    decay_ref,
    carried_hbm,
    gain_ref,
    out_ref,
    query,
    key,
    value,
    state_out,
    state_in,
    own_state,
    sums,
    chain_out,
    chain_in,
    enter_out,
    enter_in,
    logs_out,
    logs_in,
    combined,
    squares_out,
    squares_in,
    load_sem,
    state_send,
    state_recv,
    chain_send,
    chain_recv,
    enter_send,
    enter_recv,
    small_send,
    small_recv,
):
    heads, tokens = decay_ref.shape
    half = heads // 2
    width = query.shape[1] // heads
    seq = lax.axis_index("seq")
    tp = lax.axis_index("tp")
    side = lax.rem(seq, 2)
    pair = lax.div(seq, 2)
    partner = seq + 1 - 2 * side
    first = side == 0
    not_start = jnp.where(pair > 0, 1, 0)
    not_end = jnp.where(pair < pairs - 1, 1, 0)

    loads = [
        pltpu.make_async_copy(key_hbm, key, load_sem.at[0]),
        pltpu.make_async_copy(value_hbm, value, load_sem.at[1]),
        pltpu.make_async_copy(query_hbm, query, load_sem.at[2]),
    ]
    for load in loads:
        load.start()

    barrier = pltpu.get_barrier_semaphore()
    pl.semaphore_signal(barrier, inc=1, device_id={"seq": partner}, device_id_type=MESH)
    pl.semaphore_signal(barrier, inc=1, device_id={"tp": 1 - tp}, device_id_type=MESH)

    @pl.when(pair > 0)
    def _():
        pl.semaphore_signal(barrier, inc=1, device_id={"seq": seq - 2}, device_id_type=MESH)

    @pl.when(pair < pairs - 1)
    def _():
        pl.semaphore_signal(barrier, inc=1, device_id={"seq": seq + 2}, device_id_type=MESH)

    direct = chain_in.dtype == carried_hbm.dtype
    carried_copy = pltpu.make_async_copy(
        carried_hbm.at[pl.ds(side * half, half)], chain_in if direct else sums, load_sem.at[3]
    )

    @pl.when(pair == 0)
    def _():
        carried_copy.start()

    decay = decay_ref[...]
    decay = jnp.where(first, decay, jnp.concatenate([decay[half:], decay[:half]], axis=0))
    t_index = lax.broadcasted_iota(jnp.int32, (tokens, tokens), 0)
    s_index = lax.broadcasted_iota(jnp.int32, (tokens, tokens), 1)
    causal = s_index <= t_index
    lower = jnp.where(causal, 1.0, 0.0).astype(F32)
    contract_last = (((1,), (1,)), ((), ()))
    cumul_row = lax.dot_general(decay, lower, contract_last, precision=EXACT, preferred_element_type=F32)
    cumul_col = lax.dot_general(lower, decay, contract_last, precision=EXACT, preferred_element_type=F32)
    after_col = lax.dot_general(
        1.0 - lower, decay, contract_last, precision=EXACT, preferred_element_type=F32
    )
    total = jnp.dot(
        decay, jnp.ones((tokens, width), F32), precision=EXACT, preferred_element_type=F32
    )
    key_scale = jnp.exp(after_col)
    query_scale = jnp.exp(cumul_col)
    logs_out[...] = total

    def columns(i):
        head = lax.rem(side * half + i, heads)
        return pl.ds(pl.multiple_of(head * width, width), width)

    def send(src, dst, send_sem, recv_sem, where):
        return pltpu.make_async_remote_copy(
            src_ref=src,
            dst_ref=dst,
            send_sem=send_sem,
            recv_sem=recv_sem,
            device_id=where,
            device_id_type=MESH,
        )

    logs_copy = send(logs_out, logs_in, small_send.at[0], small_recv.at[0], {"seq": partner})
    squares_copy = send(
        squares_out, squares_in, small_send.at[1], small_recv.at[1], {"tp": 1 - tp}
    )
    state_copy = [
        send(state_out.at[i], state_in.at[i], state_send.at[i], state_recv.at[i], {"seq": partner})
        for i in range(half)
    ]
    chain_copy = [
        send(chain_out.at[i], chain_in.at[i], chain_send.at[i], chain_recv.at[i], {"seq": seq + 2})
        for i in range(half)
    ]
    enter_copy = [
        send(enter_out.at[i], enter_in.at[i], enter_send.at[i], enter_recv.at[i], {"seq": partner})
        for i in range(half)
    ]

    def block_state(i):
        at = columns(i)
        decayed = (key[:, at].astype(F32) * key_scale[:, i : i + 1]).astype(BF16)
        return lax.dot_general(
            decayed, value[:, at], (((0,), (0,)), ((), ())), preferred_element_type=F32
        ).astype(BF16)

    def mixing(i):
        at = columns(i)
        scores = lax.dot_general(
            query[:, at], key[:, at], contract_last, preferred_element_type=F32
        )
        spread = cumul_col[:, i : i + 1] - cumul_row[i : i + 1, :]
        weights = jnp.where(causal, jnp.exp(jnp.minimum(spread, 0.0)), 0.0)
        return (scores * weights).astype(BF16)

    def attend(i, mixed, entering):
        at = columns(i)
        decayed = (query[:, at].astype(F32) * query_scale[:, i : i + 1]).astype(BF16)
        left = jnp.concatenate([mixed, decayed], axis=1)
        right = jnp.concatenate([value[:, at], entering], axis=0)
        result = jnp.dot(left, right, preferred_element_type=F32)
        combined[:, at] = result
        return result * result

    pl.semaphore_wait(barrier, 2 + not_start + not_end)
    logs_copy.start()
    loads[0].wait()
    loads[1].wait()
    for i in range(half):
        state_out[i] = block_state(half + i)
        state_copy[i].start()
    for i in range(half):
        own_state[i] = block_state(i)
    loads[2].wait()
    logs_copy.wait_recv()

    @pl.when(pair == 0)
    def _():
        carried_copy.wait()
        if not direct:
            chain_in[...] = sums[...].astype(chain_in.dtype)

    own_log = total[:half]
    other_log = logs_in[half:, :]
    first_decay = jnp.exp(jnp.where(first, own_log, other_log))
    second_decay = jnp.exp(jnp.where(first, other_log, own_log))
    both_decay = jnp.exp(own_log + other_log)

    squares = jnp.zeros((tokens, width), F32)
    for i in range(half):
        state_copy[i].wait_recv()
        mine = own_state[i].astype(F32)
        theirs = state_in[i].astype(F32)
        state_first = jnp.where(first, mine, theirs)
        state_second = jnp.where(first, theirs, mine)
        both = second_decay[i : i + 1] * state_first + state_second

        @pl.when(pair > 0)
        def _():
            chain_copy[i].wait_recv()

        before = chain_in[i].astype(F32)
        chain_out[i] = (both_decay[i : i + 1] * before + both).astype(chain_out.dtype)

        @pl.when(pair < pairs - 1)
        def _():
            chain_copy[i].start()

        between = first_decay[i : i + 1] * before + state_first
        enter_out[i] = jnp.where(first, between, before).astype(BF16)
        enter_copy[i].start()
        entering = jnp.where(first, before, between).astype(BF16)
        squares = squares + attend(i, mixing(i), entering)
    for i in range(half):
        mixed = mixing(half + i)
        enter_copy[i].wait_recv()
        squares = squares + attend(half + i, mixed, enter_in[i])

    squares_out[...] = squares
    squares_copy.start()
    squares_copy.wait_recv()
    meansq = jnp.sum(squares + squares_in[...], axis=1, keepdims=True) / features
    scale = lax.rsqrt(meansq + 1e-06)
    for i in range(heads):
        at = slice(i * width, (i + 1) * width)
        out_ref[:, at] = (combined[:, at] * scale * gain_ref[:, at]).astype(BF16)

    logs_copy.wait_send()
    squares_copy.wait_send()
    for i in range(half):
        state_copy[i].wait_send()
        enter_copy[i].wait_send()

    @pl.when(pair < pairs - 1)
    def _():
        for i in range(half):
            chain_copy[i].wait_send()


def per_device(query_rows, key_rows, value_rows, log_decay, carried_state, norm_gain):
    tokens, columns = query_rows.shape
    heads, depth, width = carried_state.shape
    half = heads // 2
    devices = lax.axis_size("seq")
    chain_dtype = BF16 if devices <= 16 else F32
    block = (half, depth, width)
    vmem = pl.BlockSpec(memory_space=pltpu.VMEM)
    hbm = pl.BlockSpec(memory_space=pl.ANY)
    dma = pltpu.SemaphoreType.DMA
    return pl.pallas_call(
        functools.partial(kernel, devices // 2, columns * lax.axis_size("tp")),
        out_shape=jax.ShapeDtypeStruct((tokens, columns), BF16),
        in_specs=[hbm, hbm, hbm, vmem, hbm, vmem],
        out_specs=vmem,
        scratch_shapes=[
            pltpu.VMEM((tokens, columns), BF16),
            pltpu.VMEM((tokens, columns), BF16),
            pltpu.VMEM((tokens, columns), BF16),
            pltpu.VMEM(block, BF16),
            pltpu.VMEM(block, BF16),
            pltpu.VMEM(block, BF16),
            pltpu.VMEM(block, BF16),
            pltpu.VMEM(block, chain_dtype),
            pltpu.VMEM(block, chain_dtype),
            pltpu.VMEM(block, BF16),
            pltpu.VMEM(block, BF16),
            pltpu.VMEM((heads, width), F32),
            pltpu.VMEM((heads, width), F32),
            pltpu.VMEM((tokens, columns), F32),
            pltpu.VMEM((tokens, width), F32),
            pltpu.VMEM((tokens, width), F32),
            dma((4,)),
            dma((half,)),
            dma((half,)),
            dma((half,)),
            dma((half,)),
            dma((half,)),
            dma((half,)),
            dma((2,)),
            dma((2,)),
        ],
        compiler_params=pltpu.CompilerParams(
            collective_id=0, has_side_effects=True, vmem_limit_bytes=63 * 1024 * 1024
        ),
    )(query_rows, key_rows, value_rows, log_decay, carried_state, norm_gain.reshape(1, columns))


def solution(mesh):
    in_specs = (
        P(("groups", "seq"), "tp"),
        P(("groups", "seq"), "tp"),
        P(("groups", "seq"), "tp"),
        P("tp", ("groups", "seq")),
        P(("groups", "tp"), None, None),
        P("tp"),
    )
    return jax.shard_map(
        per_device,
        mesh=mesh,
        in_specs=in_specs,
        out_specs=P(("groups", "seq"), "tp"),
        check_vma=False,
    )
```

```python
import functools

import jax
import jax.numpy as jnp
from jax import lax
from jax.experimental import pallas as pl
from jax.experimental.pallas import tpu as pltpu
from jax.sharding import PartitionSpec as P

MESH = pl.DeviceIdType.MESH
F32 = jnp.float32
BF16 = jnp.bfloat16
EXACT = lax.Precision.HIGHEST


def kernel(
    pairs,
    features,
    query_hbm,
    key_hbm,
    value_hbm,
    decay_hbm,
    carried_hbm,
    gain_hbm,
    out_ref,
    query,
    key,
    value,
    decay_ref,
    gain_ref,
    state_out,
    state_in,
    own_state,
    sums,
    chain_out,
    chain_in,
    enter_out,
    enter_in,
    logs_out,
    logs_in,
    combined,
    squares_out,
    squares_in,
    load_sem,
    state_send,
    state_recv,
    chain_send,
    chain_recv,
    enter_send,
    enter_recv,
    small_send,
    small_recv,
):
    heads, tokens = decay_ref.shape
    half = heads // 2
    width = query.shape[1] // heads
    seq = lax.axis_index("seq")
    tp = lax.axis_index("tp")
    side = lax.rem(seq, 2)
    pair = lax.div(seq, 2)
    partner = seq + 1 - 2 * side
    first = side == 0
    not_start = jnp.where(pair > 0, 1, 0)
    not_end = jnp.where(pair < pairs - 1, 1, 0)

    barrier = pltpu.get_barrier_semaphore()
    pl.semaphore_signal(barrier, inc=1, device_id={"seq": partner}, device_id_type=MESH)
    pl.semaphore_signal(barrier, inc=1, device_id={"tp": 1 - tp}, device_id_type=MESH)

    @pl.when(pair > 0)
    def _():
        pl.semaphore_signal(barrier, inc=1, device_id={"seq": seq - 2}, device_id_type=MESH)

    @pl.when(pair < pairs - 1)
    def _():
        pl.semaphore_signal(barrier, inc=1, device_id={"seq": seq + 2}, device_id_type=MESH)

    decay_load = pltpu.make_async_copy(decay_hbm, decay_ref, load_sem.at[5])
    decay_load.start()
    loads = [
        pltpu.make_async_copy(key_hbm, key, load_sem.at[0]),
        pltpu.make_async_copy(value_hbm, value, load_sem.at[1]),
        pltpu.make_async_copy(query_hbm, query, load_sem.at[2]),
        pltpu.make_async_copy(gain_hbm, gain_ref, load_sem.at[4]),
    ]
    for load in loads:
        load.start()

    direct = chain_in.dtype == carried_hbm.dtype
    carried_copy = pltpu.make_async_copy(
        carried_hbm.at[pl.ds(side * half, half)], chain_in if direct else sums, load_sem.at[3]
    )

    @pl.when(pair == 0)
    def _():
        carried_copy.start()

    decay_load.wait()
    decay = decay_ref[...]
    decay = jnp.where(first, decay, jnp.concatenate([decay[half:], decay[:half]], axis=0))
    t_index = lax.broadcasted_iota(jnp.int32, (tokens, tokens), 0)
    s_index = lax.broadcasted_iota(jnp.int32, (tokens, tokens), 1)
    causal = s_index <= t_index
    lower = jnp.where(causal, 1.0, 0.0).astype(F32)
    contract_last = (((1,), (1,)), ((), ()))
    cumul_row = lax.dot_general(decay, lower, contract_last, precision=EXACT, preferred_element_type=F32)
    cumul_col = lax.dot_general(lower, decay, contract_last, precision=EXACT, preferred_element_type=F32)
    after_col = lax.dot_general(
        1.0 - lower, decay, contract_last, precision=EXACT, preferred_element_type=F32
    )
    total = jnp.dot(
        decay, jnp.ones((tokens, width), F32), precision=EXACT, preferred_element_type=F32
    )
    key_scale = jnp.exp(after_col)
    query_scale = jnp.exp(cumul_col)
    logs_out[...] = total

    def columns(i):
        head = lax.rem(side * half + i, heads)
        return pl.ds(pl.multiple_of(head * width, width), width)

    def send(src, dst, send_sem, recv_sem, where):
        return pltpu.make_async_remote_copy(
            src_ref=src,
            dst_ref=dst,
            send_sem=send_sem,
            recv_sem=recv_sem,
            device_id=where,
            device_id_type=MESH,
        )

    logs_copy = send(logs_out, logs_in, small_send.at[0], small_recv.at[0], {"seq": partner})
    squares_copy = send(
        squares_out, squares_in, small_send.at[1], small_recv.at[1], {"tp": 1 - tp}
    )
    state_copy = [
        send(state_out.at[i], state_in.at[i], state_send.at[i], state_recv.at[i], {"seq": partner})
        for i in range(half)
    ]
    chain_copy = [
        send(chain_out.at[i], chain_in.at[i], chain_send.at[i], chain_recv.at[i], {"seq": seq + 2})
        for i in range(half)
    ]
    enter_copy = [
        send(enter_out.at[i], enter_in.at[i], enter_send.at[i], enter_recv.at[i], {"seq": partner})
        for i in range(half)
    ]

    def block_state(i):
        at = columns(i)
        decayed = (key[:, at].astype(F32) * key_scale[:, i : i + 1]).astype(BF16)
        return lax.dot_general(
            decayed, value[:, at], (((0,), (0,)), ((), ())), preferred_element_type=F32
        ).astype(BF16)

    def mixing(i):
        at = columns(i)
        scores = lax.dot_general(
            query[:, at], key[:, at], contract_last, preferred_element_type=F32
        )
        spread = cumul_col[:, i : i + 1] - cumul_row[i : i + 1, :]
        weights = jnp.where(causal, jnp.exp(jnp.minimum(spread, 0.0)), 0.0)
        return (scores * weights).astype(BF16)

    def attend(i, mixed, entering):
        at = columns(i)
        decayed = (query[:, at].astype(F32) * query_scale[:, i : i + 1]).astype(BF16)
        left = jnp.concatenate([mixed, decayed], axis=1)
        right = jnp.concatenate([value[:, at], entering], axis=0)
        result = jnp.dot(left, right, preferred_element_type=F32)
        combined[:, at] = result
        return result * result

    pl.semaphore_wait(barrier, 2 + not_start + not_end)
    logs_copy.start()
    loads[0].wait()
    loads[1].wait()
    for i in range(half):
        state_out[i] = block_state(half + i)
        state_copy[i].start()
    for i in range(half):
        own_state[i] = block_state(i)
    loads[2].wait()
    logs_copy.wait_recv()

    @pl.when(pair == 0)
    def _():
        carried_copy.wait()
        if not direct:
            chain_in[...] = sums[...].astype(chain_in.dtype)

    own_log = total[:half]
    other_log = logs_in[half:, :]
    first_decay = jnp.exp(jnp.where(first, own_log, other_log))
    second_decay = jnp.exp(jnp.where(first, other_log, own_log))
    both_decay = jnp.exp(own_log + other_log)

    squares = jnp.zeros((tokens, width), F32)
    for i in range(half):
        state_copy[i].wait_recv()
        mine = own_state[i].astype(F32)
        theirs = state_in[i].astype(F32)
        state_first = jnp.where(first, mine, theirs)
        state_second = jnp.where(first, theirs, mine)
        both = second_decay[i : i + 1] * state_first + state_second

        @pl.when(pair > 0)
        def _():
            chain_copy[i].wait_recv()

        before = chain_in[i].astype(F32)
        chain_out[i] = (both_decay[i : i + 1] * before + both).astype(chain_out.dtype)

        @pl.when(pair < pairs - 1)
        def _():
            chain_copy[i].start()

        between = first_decay[i : i + 1] * before + state_first
        enter_out[i] = jnp.where(first, between, before).astype(BF16)

        @pl.when(pair > 0)
        def _():
            enter_copy[i].start()

        entering = jnp.where(first, before, between).astype(BF16)
        squares = squares + attend(i, mixing(i), entering)

    @pl.when(pair == 0)
    def _():
        for i in range(half):
            enter_copy[i].start()

    for i in range(half):
        mixed = mixing(half + i)
        enter_copy[i].wait_recv()
        squares = squares + attend(half + i, mixed, enter_in[i])

    squares_out[...] = squares
    squares_copy.start()
    squares_copy.wait_recv()
    loads[3].wait()
    meansq = jnp.sum(squares + squares_in[...], axis=1, keepdims=True) / features
    scale = lax.rsqrt(meansq + 1e-06)
    for i in range(heads):
        at = slice(i * width, (i + 1) * width)
        out_ref[:, at] = (combined[:, at] * scale * gain_ref[:, at]).astype(BF16)

    logs_copy.wait_send()
    squares_copy.wait_send()
    for i in range(half):
        state_copy[i].wait_send()
        enter_copy[i].wait_send()

    @pl.when(pair < pairs - 1)
    def _():
        for i in range(half):
            chain_copy[i].wait_send()


def per_device(query_rows, key_rows, value_rows, log_decay, carried_state, norm_gain):
    tokens, columns = query_rows.shape
    heads, depth, width = carried_state.shape
    half = heads // 2
    devices = lax.axis_size("seq")
    chain_dtype = BF16 if devices <= 16 else F32
    block = (half, depth, width)
    vmem = pl.BlockSpec(memory_space=pltpu.VMEM)
    hbm = pl.BlockSpec(memory_space=pl.ANY)
    dma = pltpu.SemaphoreType.DMA
    return pl.pallas_call(
        functools.partial(kernel, devices // 2, columns * lax.axis_size("tp")),
        out_shape=pltpu.VMEM((tokens, columns), BF16),
        in_specs=[hbm] * 6,
        out_specs=vmem,
        scratch_shapes=[
            pltpu.VMEM((tokens, columns), BF16),
            pltpu.VMEM((tokens, columns), BF16),
            pltpu.VMEM((tokens, columns), BF16),
            pltpu.VMEM((heads, tokens), F32),
            pltpu.VMEM((1, columns), F32),
            pltpu.VMEM(block, BF16),
            pltpu.VMEM(block, BF16),
            pltpu.VMEM(block, BF16),
            pltpu.VMEM(block, BF16),
            pltpu.VMEM(block, chain_dtype),
            pltpu.VMEM(block, chain_dtype),
            pltpu.VMEM(block, BF16),
            pltpu.VMEM(block, BF16),
            pltpu.VMEM((heads, width), F32),
            pltpu.VMEM((heads, width), F32),
            pltpu.VMEM((tokens, columns), F32),
            pltpu.VMEM((tokens, width), F32),
            pltpu.VMEM((tokens, width), F32),
            dma((6,)),
            dma((half,)),
            dma((half,)),
            dma((half,)),
            dma((half,)),
            dma((half,)),
            dma((half,)),
            dma((2,)),
            dma((2,)),
        ],
        compiler_params=pltpu.CompilerParams(
            collective_id=0, has_side_effects=True, vmem_limit_bytes=56 * 1024 * 1024
        ),
    )(query_rows, key_rows, value_rows, log_decay, carried_state, norm_gain.reshape(1, columns))


def solution(mesh):
    in_specs = (
        P(("groups", "seq"), "tp"),
        P(("groups", "seq"), "tp"),
        P(("groups", "seq"), "tp"),
        P("tp", ("groups", "seq")),
        P(("groups", "tp"), None, None),
        P("tp"),
    )
    return jax.shard_map(
        per_device,
        mesh=mesh,
        in_specs=in_specs,
        out_specs=P(("groups", "seq"), "tp"),
        check_vma=False,
    )
```

```python
import functools

import jax
import jax.numpy as jnp
from jax import lax
from jax.experimental import pallas as pl
from jax.experimental.pallas import tpu as pltpu
from jax.sharding import PartitionSpec as P

MESH = pl.DeviceIdType.MESH
F32 = jnp.float32
BF16 = jnp.bfloat16
EARLY = 2
EXACT = lax.Precision.HIGHEST


def kernel(
    pairs,
    features,
    query_hbm,
    key_hbm,
    value_hbm,
    decay_hbm,
    carried_hbm,
    gain_hbm,
    out_ref,
    query,
    key,
    value,
    decay_ref,
    gain_ref,
    state_out,
    state_in,
    own_state,
    sums,
    chain_out,
    chain_in,
    enter_out,
    enter_in,
    mixed,
    logs_out,
    logs_in,
    combined,
    squares_out,
    squares_in,
    load_sem,
    state_send,
    state_recv,
    chain_send,
    chain_recv,
    enter_send,
    enter_recv,
    small_send,
    small_recv,
):
    heads, tokens = decay_ref.shape
    half = heads // 2
    width = query.shape[1] // heads
    seq = lax.axis_index("seq")
    tp = lax.axis_index("tp")
    side = lax.rem(seq, 2)
    pair = lax.div(seq, 2)
    partner = seq + 1 - 2 * side
    first = side == 0
    not_start = jnp.where(pair > 0, 1, 0)
    not_end = jnp.where(pair < pairs - 1, 1, 0)

    barrier = pltpu.get_barrier_semaphore()
    pl.semaphore_signal(barrier, inc=1, device_id={"seq": partner}, device_id_type=MESH)
    pl.semaphore_signal(barrier, inc=1, device_id={"tp": 1 - tp}, device_id_type=MESH)

    @pl.when(pair > 0)
    def _():
        pl.semaphore_signal(barrier, inc=1, device_id={"seq": seq - 2}, device_id_type=MESH)

    @pl.when(pair < pairs - 1)
    def _():
        pl.semaphore_signal(barrier, inc=1, device_id={"seq": seq + 2}, device_id_type=MESH)

    decay_load = pltpu.make_async_copy(decay_hbm, decay_ref, load_sem.at[5])
    decay_load.start()
    loads = [
        pltpu.make_async_copy(key_hbm, key, load_sem.at[0]),
        pltpu.make_async_copy(value_hbm, value, load_sem.at[1]),
        pltpu.make_async_copy(query_hbm, query, load_sem.at[2]),
        pltpu.make_async_copy(gain_hbm, gain_ref, load_sem.at[4]),
    ]
    for load in loads:
        load.start()

    direct = chain_in.dtype == carried_hbm.dtype
    carried_copy = pltpu.make_async_copy(
        carried_hbm.at[pl.ds(side * half, half)], chain_in if direct else sums, load_sem.at[3]
    )

    @pl.when(pair == 0)
    def _():
        carried_copy.start()

    decay_load.wait()
    decay = decay_ref[...]
    decay = jnp.where(first, decay, jnp.concatenate([decay[half:], decay[:half]], axis=0))
    t_index = lax.broadcasted_iota(jnp.int32, (tokens, tokens), 0)
    s_index = lax.broadcasted_iota(jnp.int32, (tokens, tokens), 1)
    causal = s_index <= t_index
    lower = jnp.where(causal, 1.0, 0.0).astype(F32)
    contract_last = (((1,), (1,)), ((), ()))
    cumul_row = lax.dot_general(decay, lower, contract_last, precision=EXACT, preferred_element_type=F32)
    cumul_col = lax.dot_general(lower, decay, contract_last, precision=EXACT, preferred_element_type=F32)
    after_col = lax.dot_general(
        1.0 - lower, decay, contract_last, precision=EXACT, preferred_element_type=F32
    )
    total = jnp.dot(
        decay, jnp.ones((tokens, width), F32), precision=EXACT, preferred_element_type=F32
    )
    key_scale = jnp.exp(after_col)
    query_scale = jnp.exp(cumul_col)
    logs_out[...] = total

    def columns(i):
        head = lax.rem(side * half + i, heads)
        return pl.ds(pl.multiple_of(head * width, width), width)

    def send(src, dst, send_sem, recv_sem, where):
        return pltpu.make_async_remote_copy(
            src_ref=src,
            dst_ref=dst,
            send_sem=send_sem,
            recv_sem=recv_sem,
            device_id=where,
            device_id_type=MESH,
        )

    logs_copy = send(logs_out, logs_in, small_send.at[0], small_recv.at[0], {"seq": partner})
    squares_copy = send(
        squares_out, squares_in, small_send.at[1], small_recv.at[1], {"tp": 1 - tp}
    )
    state_copy = [
        send(state_out.at[i], state_in.at[i], state_send.at[i], state_recv.at[i], {"seq": partner})
        for i in range(half)
    ]
    chain_copy = [
        send(chain_out.at[i], chain_in.at[i], chain_send.at[i], chain_recv.at[i], {"seq": seq + 2})
        for i in range(half)
    ]
    enter_copy = [
        send(enter_out.at[i], enter_in.at[i], enter_send.at[i], enter_recv.at[i], {"seq": partner})
        for i in range(half)
    ]

    def block_state(i):
        at = columns(i)
        decayed = (key[:, at].astype(F32) * key_scale[:, i : i + 1]).astype(BF16)
        return lax.dot_general(
            decayed, value[:, at], (((0,), (0,)), ((), ())), preferred_element_type=F32
        ).astype(BF16)

    def mixing(i):
        at = columns(i)
        scores = lax.dot_general(
            query[:, at], key[:, at], contract_last, preferred_element_type=F32
        )
        spread = cumul_col[:, i : i + 1] - cumul_row[i : i + 1, :]
        weights = jnp.where(causal, jnp.exp(jnp.minimum(spread, 0.0)), 0.0)
        return (scores * weights).astype(BF16)

    def attend(i, entering):
        at = columns(i)
        decayed = (query[:, at].astype(F32) * query_scale[:, i : i + 1]).astype(BF16)
        left = jnp.concatenate([mixed[i], decayed], axis=1)
        right = jnp.concatenate([value[:, at], entering], axis=0)
        result = jnp.dot(left, right, preferred_element_type=F32)
        combined[:, at] = result * gain_ref[:, at]
        return result * result

    pl.semaphore_wait(barrier, 2 + not_start + not_end)
    logs_copy.start()
    loads[0].wait()
    loads[1].wait()
    for i in range(half):
        state_out[i] = block_state(half + i)
        state_copy[i].start()
    for i in range(half):
        own_state[i] = block_state(i)
    loads[2].wait()
    loads[3].wait()
    logs_copy.wait_recv()

    @pl.when(pair == 0)
    def _():
        carried_copy.wait()
        if not direct:
            chain_in[...] = sums[...].astype(chain_in.dtype)

    @pl.when(pair >= EARLY)
    def _():
        for i in range(heads):
            mixed[i] = mixing(i)

    own_log = total[:half]
    other_log = logs_in[half:, :]
    first_decay = jnp.exp(jnp.where(first, own_log, other_log))
    second_decay = jnp.exp(jnp.where(first, other_log, own_log))
    both_decay = jnp.exp(own_log + other_log)

    squares = jnp.zeros((tokens, width), F32)
    for i in range(half):
        state_copy[i].wait_recv()
        mine = own_state[i].astype(F32)
        theirs = state_in[i].astype(F32)
        state_first = jnp.where(first, mine, theirs)
        state_second = jnp.where(first, theirs, mine)
        both = second_decay[i : i + 1] * state_first + state_second

        @pl.when(pair > 0)
        def _():
            chain_copy[i].wait_recv()

        before = chain_in[i].astype(F32)
        chain_out[i] = (both_decay[i : i + 1] * before + both).astype(chain_out.dtype)

        @pl.when(pair < pairs - 1)
        def _():
            chain_copy[i].start()

        between = first_decay[i : i + 1] * before + state_first
        enter_out[i] = jnp.where(first, between, before).astype(BF16)

        @pl.when(pair > 0)
        def _():
            enter_copy[i].start()

        own_state[i] = jnp.where(first, before, between).astype(BF16)

    @pl.when(pair == 0)
    def _():
        for i in range(half):
            enter_copy[i].start()

    @pl.when(pair < EARLY)
    def _():
        for i in range(heads):
            mixed[i] = mixing(i)

    for i in range(half):
        squares = squares + attend(i, own_state[i])
    for i in range(half):
        enter_copy[i].wait_recv()
        squares = squares + attend(half + i, enter_in[i])

    squares_out[...] = squares
    squares_copy.start()
    squares_copy.wait_recv()
    meansq = jnp.sum(squares + squares_in[...], axis=1, keepdims=True) / features
    scale = lax.rsqrt(meansq + 1e-06)
    for i in range(heads):
        at = slice(i * width, (i + 1) * width)
        out_ref[:, at] = (combined[:, at] * scale).astype(BF16)

    logs_copy.wait_send()
    squares_copy.wait_send()
    for i in range(half):
        state_copy[i].wait_send()
        enter_copy[i].wait_send()

    @pl.when(pair < pairs - 1)
    def _():
        for i in range(half):
            chain_copy[i].wait_send()


def per_device(query_rows, key_rows, value_rows, log_decay, carried_state, norm_gain):
    tokens, columns = query_rows.shape
    heads, depth, width = carried_state.shape
    half = heads // 2
    devices = lax.axis_size("seq")
    chain_dtype = BF16 if devices <= 16 else F32
    block = (half, depth, width)
    vmem = pl.BlockSpec(memory_space=pltpu.VMEM)
    hbm = pl.BlockSpec(memory_space=pl.ANY)
    dma = pltpu.SemaphoreType.DMA
    return pl.pallas_call(
        functools.partial(kernel, devices // 2, columns * lax.axis_size("tp")),
        out_shape=pltpu.VMEM((tokens, columns), BF16),
        in_specs=[hbm] * 6,
        out_specs=vmem,
        scratch_shapes=[
            pltpu.VMEM((tokens, columns), BF16),
            pltpu.VMEM((tokens, columns), BF16),
            pltpu.VMEM((tokens, columns), BF16),
            pltpu.VMEM((heads, tokens), F32),
            pltpu.VMEM((1, columns), F32),
            pltpu.VMEM(block, BF16),
            pltpu.VMEM(block, BF16),
            pltpu.VMEM(block, BF16),
            pltpu.VMEM(block, BF16),
            pltpu.VMEM(block, chain_dtype),
            pltpu.VMEM(block, chain_dtype),
            pltpu.VMEM(block, BF16),
            pltpu.VMEM(block, BF16),
            pltpu.VMEM((heads, tokens, tokens), BF16),
            pltpu.VMEM((heads, width), F32),
            pltpu.VMEM((heads, width), F32),
            pltpu.VMEM((tokens, columns), F32),
            pltpu.VMEM((tokens, width), F32),
            pltpu.VMEM((tokens, width), F32),
            dma((6,)),
            dma((half,)),
            dma((half,)),
            dma((half,)),
            dma((half,)),
            dma((half,)),
            dma((half,)),
            dma((2,)),
            dma((2,)),
        ],
        compiler_params=pltpu.CompilerParams(
            collective_id=0, has_side_effects=True, vmem_limit_bytes=56 * 1024 * 1024
        ),
    )(query_rows, key_rows, value_rows, log_decay, carried_state, norm_gain.reshape(1, columns))


def solution(mesh):
    in_specs = (
        P(("groups", "seq"), "tp"),
        P(("groups", "seq"), "tp"),
        P(("groups", "seq"), "tp"),
        P("tp", ("groups", "seq")),
        P(("groups", "tp"), None, None),
        P("tp"),
    )
    return jax.shard_map(
        per_device,
        mesh=mesh,
        in_specs=in_specs,
        out_specs=P(("groups", "seq"), "tp"),
        check_vma=False,
    )
```
